128 devices in a mesh: outer: 8 (over y, x_lo), inner: 16 (over z, x_hi, core).
Axes of the slice: x: 4 (x_hi: 2, x_lo: 2; x = x_hi * 2 + x_lo), y: 4, z: 4, core: 2. Of those that a mesh axis runs over, the one named last changes fastest.
Arguments:
- activations: bfloat16 [32768, 8192], P(('outer', 'inner')), may hold values from -6 to 6
- out_grads: bfloat16 [32768, 8192], P(('outer', 'inner')), may hold values from -0.75 to 0.75
- proj_in: bfloat16 [8192, 64], replicated, may hold values from -0.0625 to 0.0625
- proj_out: bfloat16 [8192, 32], replicated, may hold values from -0.0625 to 0.0625
- lengths: int32 [2048], P(('outer', 'inner')), may hold values from 1 to 16
- factor: bfloat16 [2048, 2048], P('inner'), may hold values from -0.125 to 0.125
- store: bfloat16 [393216, 2048], P(('outer', 'inner')), may hold values from -0.125 to 0.125
Outputs:
- scores: bfloat16 [1024, 393216], P(None, ('outer', 'inner'))
The draws below stay inside these ranges and needn't reach their ends.
All inputs are finite; a program needn't handle non-finite values.
Results may differ from the reference program's by a relative error of at most 0.008.
Values may be sent and summed in bfloat16 or wider, within the bound.
A program may use at most 128 MiB of HBM per device.

```python
import jax
import jax.numpy as jnp
from jax import lax

D = 8192
RIN = 64
ROUT = 32
K = 2048
SEQ_LEN = 16
STORE_DEV = 3072
NPAIR = 1024
NSEQ = 2048
TOKENS = 32768
NSTORE = 393216
DEVICES = 128


def with_ends(entries, stream_key, smallest, top_value):
    extent = entries.shape
    spot = [jax.random.randint(jax.random.fold_in(stream_key, axis), (), 0, extent[axis]) for axis in range(len(extent))]
    entries = entries.at[tuple(spot)].set(smallest)
    longest = extent.index(max(extent))
    spot[longest] = (spot[longest] + 1) % extent[longest]
    return entries.at[tuple(spot)].set(top_value)


def levels(key, dims, shards, smallest, top_value):
    level = 1.0
    for dim, blocks in shards:
        steps = jax.random.uniform(jax.random.fold_in(jax.random.fold_in(key, 6), dim), (blocks,), jnp.float32, smallest / len(shards), top_value / len(shards))
        level = level * jnp.repeat(jnp.exp(steps), dims[dim] // blocks).reshape((-1,) + (1,) * (len(dims) - 1 - dim))
    return level


def centred(own_key, extent, spread, reach, split=(), kind=jnp.bfloat16):
    values = jax.random.normal(own_key, extent, jnp.float32) * spread
    if len(split) > 0:
        values = levels(own_key, extent, split, -0.22, 0.18) * values
    return jnp.clip(values, min=-reach, max=reach).astype(kind)


def setup_inputs(seed: int = 0) -> dict:
    splits = jax.random.split(jax.random.key(seed), 8)
    activations = centred(splits[0], (TOKENS, D), 1.0, 6.0, ((0, 128),))
    out_grads = centred(splits[1], (TOKENS, D), 0.125, 0.75, ((0, 128),))
    proj_in = centred(splits[2], (D, RIN), D ** -0.5, 0.0625)
    proj_out = centred(splits[3], (D, ROUT), D ** -0.5, 0.0625)
    lengths = with_ends(jax.random.randint(splits[4], (NSEQ,), 1, SEQ_LEN + 1), jax.random.fold_in(splits[4], 1), 1, SEQ_LEN).astype(jnp.int32)
    factor = centred(splits[5], (K, K), K ** -0.5, 0.125, ((0, 16),))
    store = centred(splits[6], (NSTORE, K), K ** -0.5, 0.125, ((0, 128),))
    return {"activations": activations, "out_grads": out_grads, "proj_in": proj_in, "proj_out": proj_out, "lengths": lengths, "factor": factor, "store": store}


def reference(activations, out_grads, proj_in, proj_out, lengths, factor, store):
    in_proj = jnp.dot(activations, proj_in, preferred_element_type=jnp.float32).astype(jnp.bfloat16)
    out_full = jnp.dot(out_grads, proj_out, preferred_element_type=jnp.float32)
    index = jnp.arange(TOKENS, dtype=jnp.int32)
    position = index % SEQ_LEN
    sequence = index // SEQ_LEN
    keep = position < lengths[sequence]
    out_proj = jnp.where(keep[:, None], out_full, 0.0).astype(jnp.bfloat16)
    left = out_proj.reshape(NPAIR, 2 * SEQ_LEN, ROUT).astype(jnp.float32)
    right = in_proj.reshape(NPAIR, 2 * SEQ_LEN, RIN).astype(jnp.float32)
    pair_grads = jnp.einsum("pta,ptb->pab", left, right).reshape(NPAIR, K).astype(jnp.bfloat16)
    queries = jnp.dot(pair_grads, factor, preferred_element_type=jnp.float32).astype(jnp.bfloat16)
    blocks = store.reshape(DEVICES, STORE_DEV, K)

    def score_block(rows):
        return lax.dot_general(queries, rows, (((1,), (1,)), ((), ())), preferred_element_type=jnp.float32).astype(jnp.bfloat16)

    parts = lax.map(score_block, blocks)
    return jnp.transpose(parts, (1, 0, 2)).reshape(NPAIR, NSTORE)
```

```python
import functools

import jax
import jax.numpy as jnp
from jax import lax
from jax.experimental import pallas as pl
from jax.experimental.pallas import tpu as pltpu
from jax.sharding import PartitionSpec as P

D = 8192
RIN = 64
ROUT = 32
K = 2048
SEQ = 16
TOK = 256
NSEQ = 16
NP = 8
COLS = 128
CHUNK = 1024
NCHUNK = D // CHUNK
BF = jnp.bfloat16
F32 = jnp.float32
MESH = pl.DeviceIdType.MESH

PARTS = ((0, 48, "zxy"), (48, 48, "xyz"), (96, 32, "yzx"))


def device(pos, core):
    outer = pos["y"] * 2 + lax.rem(pos["x"], 2)
    inner = (pos["z"] * 2 + lax.div(pos["x"], 2)) * 2 + core
    return outer, inner


def gather_kernel(act, grad, w_in, w_out, lengths_hbm, factor, store, q0, q1, q2, store_v,
                  act_v, grad_v, w_in_v, w_out_v, fcol, pg, lengths,
                  load_sem, store_sem, length_sem, own_f_sem, f_send, f_recv, p_send, p_recv, s_send, s_recv,
                  g1_send, g1_recv, g2_send, g2_recv, g3_send, g3_recv, c_send, c_recv):
    qs = (q0, q1, q2)
    outer = lax.axis_index("outer")
    inner = lax.axis_index("inner")
    core = lax.rem(inner, 2)
    spot = lax.div(inner, 2)
    pos = {"y": lax.div(outer, 2), "z": lax.div(inner, 4), "x": lax.rem(spot, 2) * 2 + lax.rem(outer, 2)}
    sibling = (outer, spot * 2 + 1 - core)

    def near(axis, step):
        moved = dict(pos)
        moved[axis] = lax.rem(pos[axis] + step, 4)
        return device(moved, core)

    length_copy = pltpu.make_async_copy(lengths_hbm, lengths, length_sem)
    length_copy.start()
    loads = []
    for k in range(NCHUNK):
        cols = pl.ds(k * CHUNK, CHUNK)
        row = []
        for n, (src, dst) in enumerate(((w_in, w_in_v), (act, act_v), (w_out, w_out_v), (grad, grad_v))):
            copy = pltpu.make_async_copy(src.at[:, cols], dst.at[:, cols], load_sem.at[k, n])
            copy.start()
            row.append(copy)
        loads.append(row)

    store_copy = pltpu.make_async_copy(store, store_v, store_sem)
    store_copy.start()

    barrier = pltpu.get_barrier_semaphore()
    peers = [(outer, lax.rem(inner + k, 16)) for k in range(1, 16)]
    peers += [near("y", 1), near("y", 2), near("y", 3), near("x", 1), near("x", 3)]
    for peer in peers:
        pl.semaphore_signal(barrier, inc=1, device_id=peer, device_id_type=MESH)
    pl.semaphore_wait(barrier, len(peers))

    def remote(src, dst, send, recv, target):
        return pltpu.make_async_remote_copy(src_ref=src, dst_ref=dst, send_sem=send, recv_sem=recv,
                                            device_id=target, device_id_type=MESH)

    def columns(who):
        return factor.at[:, pl.ds(pl.multiple_of(who * COLS, COLS), COLS)]

    f_copies = []
    for k in range(1, 16):
        to = lax.rem(inner + k, 16)
        copy = remote(columns(to), fcol.at[inner], f_send.at[k], f_recv.at[k], (outer, to))
        copy.start()
        f_copies.append(copy)
    own_f = pltpu.make_async_copy(columns(inner), fcol.at[inner], own_f_sem)
    own_f.start()

    ins = jnp.zeros((TOK, 2 * RIN), F32)
    outs = jnp.zeros((TOK, ROUT), F32)
    across = (((1,), (1,)), ((), ()))
    for k in range(NCHUNK):
        cols = pl.ds(k * CHUNK, CHUNK)
        for copy in loads[k]:
            copy.wait()
        w = w_in_v[:, cols]
        ins += lax.dot_general(act_v[:, cols], jnp.concatenate([w, w], axis=0), across, preferred_element_type=F32)
        outs += lax.dot_general(grad_v[:, cols], w_out_v[:, cols], across, preferred_element_type=F32)

    length_copy.wait()
    position = lax.broadcasted_iota(jnp.int32, (SEQ, ROUT), 0)
    kept = [jnp.where(position < lengths[s], outs[s * SEQ:(s + 1) * SEQ], 0.0) for s in range(NSEQ)]
    outs = jnp.concatenate(kept, axis=0).astype(BF)
    ins = ins.astype(BF).astype(F32)
    for j in range(K // 128):
        a = lax.broadcasted_iota(jnp.int32, (ROUT, 128), 0)
        b = lax.broadcasted_iota(jnp.int32, (ROUT, 128), 1)
        pick = jnp.where(a == 2 * j + lax.div(b, RIN), 1.0, 0.0).astype(BF)
        wide = jnp.dot(outs, pick, preferred_element_type=F32)
        sums = jnp.sum((wide * ins).reshape(NP, 2 * SEQ, 128), axis=1)
        pg[inner, :, j * 128:(j + 1) * 128] = sums.astype(BF)

    p_copies = []
    for k in range(1, 8):
        to = lax.rem(spot + k, 8) * 2 + core
        copy = remote(pg.at[inner], pg.at[inner], p_send.at[k], p_recv.at[k], (outer, to))
        copy.start()
        p_copies.append(copy)
    s_copies = [remote(pg.at[inner], pg.at[inner], s_send.at[0], s_recv.at[0], sibling)]
    s_copies[0].start()
    for k in range(1, 8):
        p_copies[k - 1].wait_recv()
        slot = lax.rem(spot + 8 - k, 8) * 2 + core
        copy = remote(pg.at[slot], pg.at[slot], s_send.at[k], s_recv.at[k], sibling)
        copy.start()
        s_copies.append(copy)
    own_f.wait()
    for copy in f_copies:
        copy.wait_recv()
    for copy in s_copies:
        copy.wait_recv()

    white = jnp.dot(pg[...].reshape(16 * NP, K), fcol[...].reshape(K, COLS), preferred_element_type=F32).astype(BF)
    for q, (start, rows, order) in zip(qs, PARTS):
        q[core, pos[order[2]], pos[order[1]], pos[order[0]]] = white[start:start + rows]

    sends = list(p_copies) + list(f_copies) + list(s_copies)

    def go(*args):
        copy = remote(*args)
        copy.start()
        sends.append(copy)
        return copy

    def along(order, n, step):
        return lax.rem(pos[order[n]] + step, 4)

    first = []
    for p, (q, (_, _, order)) in enumerate(zip(qs, PARTS)):
        mine = q.at[core, pos[order[2]], pos[order[1]], pos[order[0]]]
        first.append([go(mine, mine, g1_send.at[p, d - 1], g1_recv.at[p, d - 1], near(order[0], d)) for d in (1, 3, 2)])

    def spread(p, axis, view, send, recv):
        halves = (pl.ds(0, 2), pl.ds(2, 2))
        copies = {}
        for name, step, half, n in (("r0", 1, 0, 0), ("l1", 3, 1, 1), ("r1", 1, 1, 2), ("l0", 3, 0, 3)):
            mine = view(0).at[halves[half]]
            copies[name] = go(mine, mine, send.at[p, n], recv.at[p, n], near(axis, step))
        return copies

    def relay(p, axis, view, send, recv, copies):
        for name, came, half, step, n in (("r0", 3, 0, 1, 4), ("l1", 1, 1, 3, 5)):
            copies[name].wait_recv()
            part = view(came).at[pl.ds(2 * half, 2)]
            copies["f" + name] = go(part, part, send.at[p, n], recv.at[p, n], near(axis, step))

    def view2(p):
        q, order = qs[p], PARTS[p][2]
        return lambda step: q.at[core, pos[order[2]], along(order, 1, step)]

    def view3(p):
        q, order = qs[p], PARTS[p][2]
        return lambda step: q.at[core, along(order, 2, step)]

    second, third, cross = [], [], []
    for p in range(3):
        for copy in first[p]:
            copy.wait_recv()
        second.append(spread(p, PARTS[p][2][1], view2(p), g2_send, g2_recv))
    for p in range(3):
        relay(p, PARTS[p][2][1], view2(p), g2_send, g2_recv, second[p])

    def over(p, step):
        part = view3(p)(step)
        cross.append(go(part, part, c_send.at[p, step], c_recv.at[p, step], sibling))

    for p in range(3):
        for name in ("r1", "l0", "fr0", "fl1"):
            second[p][name].wait_recv()
        third.append(spread(p, PARTS[p][2][2], view3(p), g3_send, g3_recv))
        over(p, 0)
    for p in range(3):
        relay(p, PARTS[p][2][2], view3(p), g3_send, g3_recv, third[p])
    for p in range(3):
        third[p]["r1"].wait_recv()
        over(p, 3)
        third[p]["l0"].wait_recv()
        over(p, 1)
    for p in range(3):
        third[p]["fr0"].wait_recv()
        third[p]["fl1"].wait_recv()
        over(p, 2)
    for copy in cross:
        copy.wait_recv()
    store_copy.wait()
    for copy in sends:
        copy.wait_send()


def score_kernel(q0, q1, q2, store, out):
    qs = (q0, q1, q2)
    rows = []
    for y in range(4):
        for xlo in range(2):
            for q, (_, _, order) in zip(qs, PARTS):
                cols = []
                for z in range(4):
                    for xhi in range(2):
                        for core in range(2):
                            at = {"x": xhi * 2 + xlo, "y": y, "z": z}
                            cols.append(q[core, at[order[2]], at[order[1]], at[order[0]]])
                rows.append(jnp.concatenate(cols, axis=1))
    lhs = jnp.concatenate(rows, axis=0)
    some = store[pl.ds(pl.multiple_of(pl.program_id(0) * 256, 256), 256), :]
    out[...] = lax.dot_general(lhs, some, (((1,), (1,)), ((), ())), preferred_element_type=F32).astype(BF)


def shards(activations, out_grads, proj_in, proj_out, lengths, factor, store):
    dma = pltpu.SemaphoreType.DMA
    hbm = pl.BlockSpec(memory_space=pltpu.HBM)
    vmem = pl.BlockSpec(memory_space=pltpu.VMEM)
    qs = pl.pallas_call(
        gather_kernel,
        out_shape=[pltpu.VMEM((2, 4, 4, 4, rows, COLS), BF) for _, rows, _ in PARTS] + [pltpu.VMEM(store.shape, BF)],
        in_specs=[hbm] * 7,
        out_specs=[vmem] * 4,
        scratch_shapes=[
            pltpu.VMEM((TOK, D), BF), pltpu.VMEM((TOK, D), BF),
            pltpu.VMEM((RIN, D), BF), pltpu.VMEM((ROUT, D), BF),
            pltpu.VMEM((16, 128, COLS), BF), pltpu.VMEM((16, NP, K), BF), pltpu.SMEM((NSEQ,), jnp.int32),
            dma((NCHUNK, 4)), dma, dma, dma, dma((16,)), dma((16,)), dma((8,)), dma((8,)), dma((8,)), dma((8,)),
            dma((3, 3)), dma((3, 3)), dma((3, 6)), dma((3, 6)), dma((3, 6)), dma((3, 6)), dma((3, 4)), dma((3, 4)),
        ],
        compiler_params=pltpu.CompilerParams(collective_id=0, has_side_effects=True, vmem_limit_bytes=32 << 20),
        name="gather",
    )(*[pltpu.with_memory_space_constraint(v, pltpu.HBM)
        for v in (activations, out_grads, proj_in.T, proj_out.T, lengths, factor, store)])
    n = store.shape[0]
    return pl.pallas_call(
        score_kernel,
        out_shape=jax.ShapeDtypeStruct((1024, n), BF),
        grid=(n // 256,),
        in_specs=[vmem] * 4,
        out_specs=pl.BlockSpec((1024, 256), lambda i: (0, i)),
        compiler_params=pltpu.CompilerParams(vmem_limit_bytes=32 << 20),
        name="score",
    )(*qs)


def solution(mesh):
    in_specs = (
        P(("outer", "inner"), None),
        P(("outer", "inner"), None),
        P(),
        P(),
        P(("outer", "inner")),
        P("inner", None),
        P(("outer", "inner"), None),
    )
    out_specs = P(None, ("outer", "inner"))
    return jax.shard_map(shards, mesh=mesh, in_specs=in_specs, out_specs=out_specs, check_vma=False)
```

```python
import jax
import jax.numpy as jnp
from jax import lax
from jax.experimental import pallas as pl
from jax.experimental.pallas import tpu as pltpu
from jax.sharding import PartitionSpec as P

D = 8192
RIN = 64
ROUT = 32
K = 2048
SEQ = 16
TOK = 256
NSEQ = 16
NP = 8
COLS = 128
HALF = 64
CHUNK = 1024
NCHUNK = D // CHUNK
STORE = 3072
WIDE = 1024
BLOCK = 512
BF = jnp.bfloat16
F32 = jnp.float32
MESH = pl.DeviceIdType.MESH
ACROSS = (((1,), (1,)), ((), ()))


def mod(a, b):
    return lax.rem(a, b)


def offset(j):
    half = j // 2
    return (half if half < 2 else 5 - half) if isinstance(j, int) else jnp.where(half < 2, half, 5 - half), j % 2


def gather_kernel(act, grad, w_in, w_out, lengths_hbm, factor, store, qa, total, store_v,
                  qb, act_v, grad_v, w_in_v, w_out_v, fcol, pg, lengths,
                  load_sem, store_sem, length_sem, own_f_sem, f_send, f_recv, p_send, p_recv, s_send, s_recv,
                  an_send, an_recv, bf_send, bf_recv, af_send, af_recv, bn_send, bn_recv,
                  ac_send, ac_recv, bc_send, bc_recv):
    outer = lax.axis_index("outer")
    inner = lax.axis_index("inner")
    core = mod(inner, 2)
    spot = lax.div(inner, 2)
    y, xlo = lax.div(outer, 2), mod(outer, 2)
    z, xhi = lax.div(spot, 2), mod(spot, 2)
    gx = mod(xlo + xhi, 2)
    sibling = (outer, spot * 2 + 1 - core)
    group_a = y * 2 + gx
    group_b = y * 2 + 1 - gx

    def near(j, flip=0):
        dz, dx = offset(j)
        hi = mod(xhi + dx, 2)
        return y * 2 + mod(gx + hi, 2), (mod(z + dz, 4) * 2 + hi) * 2 + mod(core + flip, 2)

    def near_spot(j):
        dz, dx = offset(j)
        return mod(z + 4 - dz, 4) * 2 + mod(xhi + dx, 2)

    def far(j):
        dy, dx = offset(j)
        return mod(y + dy, 4) * 2 + mod(gx + dx + xhi, 2), inner

    def far_group(j):
        dy, dx = offset(j)
        return mod(y + 4 - dy, 4) * 2 + mod(gx + dx, 2)

    length_copy = pltpu.make_async_copy(lengths_hbm, lengths, length_sem)
    length_copy.start()
    loads = []
    for k in range(NCHUNK):
        cols = pl.ds(k * CHUNK, CHUNK)
        row = []
        for n, (src, dst) in enumerate(((w_in, w_in_v), (act, act_v), (w_out, w_out_v), (grad, grad_v))):
            copy = pltpu.make_async_copy(src.at[:, cols], dst.at[:, cols], load_sem.at[k, n])
            copy.start()
            row.append(copy)
        loads.append(row)

    barrier = pltpu.get_barrier_semaphore()
    peers = [near(j, flip) for j in range(8) for flip in range(2) if j + flip] + [far(j) for j in range(1, 8)]
    for peer in peers:
        pl.semaphore_signal(barrier, inc=1, device_id=peer, device_id_type=MESH)
    total[...] = jnp.zeros(total.shape, F32)
    pl.semaphore_wait(barrier, len(peers))

    def remote(src, send, recv, target, dst=None):
        return pltpu.make_async_remote_copy(src_ref=src, dst_ref=src if dst is None else dst, send_sem=send, recv_sem=recv,
                                            device_id=target, device_id_type=MESH)

    sends = []

    def go(*args):
        copy = remote(*args)
        copy.start()
        sends.append(copy)
        return copy

    def columns(who):
        return factor.at[:, pl.ds(pl.multiple_of(who * COLS, COLS), COLS)]

    f_copies = []
    for n in range(1, 16):
        to = near(n // 2, n % 2)
        f_copies.append(go(columns(to[1]), f_send.at[n], f_recv.at[n], to, fcol.at[inner]))
    own_f = pltpu.make_async_copy(columns(inner), fcol.at[inner], own_f_sem)
    own_f.start()

    ins = jnp.zeros((TOK, 2 * RIN), F32)
    outs = jnp.zeros((TOK, ROUT), F32)
    for k in range(NCHUNK):
        cols = pl.ds(k * CHUNK, CHUNK)
        for copy in loads[k]:
            copy.wait()
        if k == NCHUNK - 1:
            store_copy = pltpu.make_async_copy(store, store_v, store_sem)
            store_copy.start()
        w = w_in_v[:, cols]
        ins += lax.dot_general(act_v[:, cols], jnp.concatenate([w, w], axis=0), ACROSS, preferred_element_type=F32)
        outs += lax.dot_general(grad_v[:, cols], w_out_v[:, cols], ACROSS, preferred_element_type=F32)

    length_copy.wait()
    position = lax.broadcasted_iota(jnp.int32, (SEQ, ROUT), 0)
    kept = [jnp.where(position < lengths[s], outs[s * SEQ:(s + 1) * SEQ], 0.0) for s in range(NSEQ)]
    outs = jnp.concatenate(kept, axis=0).astype(BF)
    ins = ins.astype(BF).astype(F32)
    own_slot = xhi * 8 + z * 2 + core
    for j in range(K // 128):
        a = lax.broadcasted_iota(jnp.int32, (ROUT, 128), 0)
        b = lax.broadcasted_iota(jnp.int32, (ROUT, 128), 1)
        pick = jnp.where(a == 2 * j + lax.div(b, RIN), 1.0, 0.0).astype(BF)
        wide = jnp.dot(outs, pick, preferred_element_type=F32)
        sums = jnp.sum((wide * ins).reshape(NP, 2 * SEQ, 128), axis=1)
        pg[own_slot, :, j * 128:(j + 1) * 128] = sums.astype(BF)

    p_copies = [go(pg.at[own_slot], p_send.at[j], p_recv.at[j], near(j)) for j in range(1, 8)]
    s_copies = [go(pg.at[own_slot], s_send.at[0], s_recv.at[0], sibling)]
    for j in range(1, 8):
        p_copies[j - 1].wait_recv()
        from_spot = near_spot(j)
        slot = mod(from_spot, 2) * 8 + lax.div(from_spot, 2) * 2 + core
        s_copies.append(go(pg.at[slot], s_send.at[j], s_recv.at[j], sibling))
    own_f.wait()
    for copy in f_copies:
        copy.wait_recv()
    for copy in s_copies:
        copy.wait_recv()

    white = jnp.dot(pg[...].reshape(16 * NP, K), fcol[...].reshape(K, COLS), preferred_element_type=F32).astype(BF)
    qa[core, group_a, spot] = white[:HALF]
    qb[core, spot, group_b] = white[HALF:]

    a_near, b_far = [], []
    for j in range(1, 8):
        a_near.append(go(qa.at[core, group_a, spot], an_send.at[j], an_recv.at[j], near(j)))
        b_far.append(go(qb.at[core, spot, group_b], bf_send.at[j], bf_recv.at[j], far(j)))

    def a_over(j):
        return remote(qa.at[core, far_group(j)], ac_send.at[j], ac_recv.at[j], sibling)

    def b_over(j):
        return remote(qb.at[core, near_spot(j)], bc_send.at[j], bc_recv.at[j], sibling)

    def a_far(j):
        return remote(qa.at[core, group_a], af_send.at[j], af_recv.at[j], far(j))

    def b_near(j):
        return remote(qb.at[core, spot], bn_send.at[j], bn_recv.at[j], near(j))

    for copy in b_far:
        copy.wait_recv()
    for j in range(1, 8):
        b_near(j).start()
    b_over(0).start()
    for copy in a_near:
        copy.wait_recv()
    for j in range(1, 8):
        a_far(j).start()
    a_over(0).start()
    store_copy.wait()

    def step(j, carry):
        @pl.when(j < 7)
        def _():
            b_near(j + 1).wait_recv()
            b_over(j + 1).start()
            a_far(j + 1).wait_recv()
            a_over(j + 1).start()

        b_over(j).wait_recv()
        k8 = near_spot(j)
        lhs = jnp.concatenate([qb[0, k8].reshape(8 * HALF, COLS), qb[1, k8].reshape(8 * HALF, COLS)], axis=1)
        cols = pl.ds(pl.multiple_of(k8 * 2 * COLS, 2 * COLS), 2 * COLS)
        for n in range(STORE // WIDE):
            some = slice(n * WIDE, (n + 1) * WIDE)
            total[:, some] += lax.dot_general(lhs, store_v[some, cols], ACROSS, preferred_element_type=F32)
        return carry

    lax.fori_loop(0, 8, step, 0)

    def finish(j, carry):
        a_over(j).wait()
        b_over(j).wait_send()

        @pl.when(j > 0)
        def _():
            a_far(j).wait_send()
            b_near(j).wait_send()
        return carry

    lax.fori_loop(0, 8, finish, 0)
    for copy in sends:
        copy.wait_send()


def score_kernel(qa, total, store, out):
    some = pl.ds(pl.multiple_of(pl.program_id(0) * BLOCK, BLOCK), BLOCK)
    rows = [jnp.concatenate([qa[c, g, k] for k in range(8) for c in range(2)], axis=1) for g in range(8)]
    lhs = jnp.concatenate(rows, axis=0)
    first = lax.dot_general(lhs, store[some, :], ACROSS, preferred_element_type=F32).astype(BF)
    second = total[:, some].astype(BF)
    for n in range(32):
        part = slice(16 * n, 16 * n + 16)
        out[32 * n:32 * n + 16, :] = first[part]
        out[32 * n + 16:32 * n + 32, :] = second[part]


def shards(activations, out_grads, proj_in, proj_out, lengths, factor, store):
    dma = pltpu.SemaphoreType.DMA
    hbm = pl.BlockSpec(memory_space=pltpu.HBM)
    vmem = pl.BlockSpec(memory_space=pltpu.VMEM)
    parts = pl.pallas_call(
        gather_kernel,
        out_shape=[pltpu.VMEM((2, 8, 8, HALF, COLS), BF), pltpu.VMEM((8 * HALF, STORE), F32), pltpu.VMEM((STORE, K), BF)],
        in_specs=[hbm] * 7,
        out_specs=[vmem] * 3,
        scratch_shapes=[
            pltpu.VMEM((2, 8, 8, HALF, COLS), BF),
            pltpu.VMEM((TOK, D), BF), pltpu.VMEM((TOK, D), BF),
            pltpu.VMEM((RIN, D), BF), pltpu.VMEM((ROUT, D), BF),
            pltpu.VMEM((16, 128, COLS), BF), pltpu.VMEM((16, NP, K), BF), pltpu.SMEM((NSEQ,), jnp.int32),
            dma((NCHUNK, 4)), dma, dma, dma, dma((16,)), dma((16,)),
        ] + [dma((8,))] * 16,
        compiler_params=pltpu.CompilerParams(collective_id=0, has_side_effects=True, vmem_limit_bytes=32 << 20),
        name="gather",
    )(*[pltpu.with_memory_space_constraint(v, pltpu.HBM)
        for v in (activations, out_grads, proj_in.T, proj_out.T, lengths, factor, store)])
    return pl.pallas_call(
        score_kernel,
        out_shape=jax.ShapeDtypeStruct((16 * HALF, STORE), BF),
        grid=(STORE // BLOCK,),
        in_specs=[vmem] * 3,
        out_specs=pl.BlockSpec((16 * HALF, BLOCK), lambda i: (0, i)),
        compiler_params=pltpu.CompilerParams(vmem_limit_bytes=32 << 20),
        name="score",
    )(*parts)


def solution(mesh):
    in_specs = (
        P(("outer", "inner"), None),
        P(("outer", "inner"), None),
        P(),
        P(),
        P(("outer", "inner")),
        P("inner", None),
        P(("outer", "inner"), None),
    )
    out_specs = P(None, ("outer", "inner"))
    return jax.shard_map(shards, mesh=mesh, in_specs=in_specs, out_specs=out_specs, check_vma=False)
```

```python
import jax
import jax.numpy as jnp
from jax import lax
from jax.experimental import pallas as pl
from jax.experimental.pallas import tpu as pltpu
from jax.sharding import PartitionSpec as P

D = 8192
RIN = 64
ROUT = 32
K = 2048
SEQ = 16
TOK = 256
NSEQ = 16
NP = 8
COLS = 128
HALF = 64
CHUNK = 1024
NCHUNK = D // CHUNK
STORE = 3072
WIDE = 1024
BF = jnp.bfloat16
F32 = jnp.float32
MESH = pl.DeviceIdType.MESH
ACROSS = (((1,), (1,)), ((), ()))


def mod(a, b):
    return lax.rem(a, b)


RING = (0, 1, 3, 2)


def offset(j):
    return RING[j // 2], j % 2


def gather_kernel(act, grad, w_in, w_out, lengths_hbm, factor, store, qb, done, early, store_v,
                  qa, total, fown, act_v, grad_v, w_in_v, w_out_v, fcol, pg, lengths,
                  load_sem, store_sem, length_sem, stage_sem, own_f_sem, f_send, f_recv, p_send, p_recv, s_send, s_recv,
                  af_send, af_recv, bn_send, bn_recv, an_send, an_recv, bf_send, bf_recv,
                  ac_send, ac_recv, bc_send, bc_recv):
    outer = lax.axis_index("outer")
    inner = lax.axis_index("inner")
    core = mod(inner, 2)
    spot = lax.div(inner, 2)
    y, xlo = lax.div(outer, 2), mod(outer, 2)
    z, xhi = lax.div(spot, 2), mod(spot, 2)
    gx = mod(xlo + xhi, 2)
    sibling = (outer, spot * 2 + 1 - core)
    member = y * 2 + gx

    def near(j, flip=0):
        dz, dx = offset(j)
        hi = mod(xhi + dx, 2)
        return y * 2 + mod(gx + hi, 2), (mod(z + dz, 4) * 2 + hi) * 2 + mod(core + flip, 2)

    def far(j):
        dy, dx = offset(j)
        return mod(y + dy, 4) * 2 + mod(gx + dx + xhi, 2), inner

    length_copy = pltpu.make_async_copy(lengths_hbm, lengths, length_sem)
    length_copy.start()
    stages = []
    for n in range(2):
        cols = pl.ds(pl.multiple_of((member * 2 + n) * COLS, COLS), COLS)
        copy = pltpu.make_async_copy(factor.at[:, cols], fown.at[n], stage_sem.at[n])
        copy.start()
        stages.append(copy)
    loads = []
    for k in range(NCHUNK):
        cols = pl.ds(k * CHUNK, CHUNK)
        row = []
        for n, (src, dst) in enumerate(((w_in, w_in_v), (act, act_v), (w_out, w_out_v), (grad, grad_v))):
            copy = pltpu.make_async_copy(src.at[:, cols], dst.at[:, cols], load_sem.at[k, n])
            copy.start()
            row.append(copy)
        loads.append(row)

    barrier = pltpu.get_barrier_semaphore()
    peers = [near(j, flip) for j in range(8) for flip in range(2) if j + flip] + [far(j) for j in range(1, 8)]
    for peer in peers:
        pl.semaphore_signal(barrier, inc=1, device_id=peer, device_id_type=MESH)
    def remote(src, send, recv, target, dst=None):
        return pltpu.make_async_remote_copy(src_ref=src, dst_ref=src if dst is None else dst, send_sem=send, recv_sem=recv,
                                            device_id=target, device_id_type=MESH)

    sends = []

    def go(*args):
        copy = remote(*args)
        copy.start()
        sends.append(copy)
        return copy

    f_copies = []
    ins = jnp.zeros((RIN, TOK), F32)
    outs = jnp.zeros((ROUT, TOK), F32)
    for k in range(NCHUNK):
        cols = pl.ds(k * CHUNK, CHUNK)
        for copy in loads[k]:
            copy.wait()
        if k == 2:
            for copy in stages:
                copy.wait()
            pl.semaphore_wait(barrier, len(peers))
            for n in range(1, 16):
                to = near(n // 2, n % 2)
                f_copies.append(go(fown.at[mod(to[1], 2)], f_send.at[n], f_recv.at[n], to, fcol.at[inner]))
            own_f = pltpu.make_async_copy(fown.at[core], fcol.at[inner], own_f_sem)
            own_f.start()
        if k == NCHUNK - 1:
            store_copy = pltpu.make_async_copy(store, store_v, store_sem)
            store_copy.start()
        ins += lax.dot_general(w_in_v[:, cols], act_v[:, cols], ACROSS, preferred_element_type=F32)
        outs += lax.dot_general(w_out_v[:, cols], grad_v[:, cols], ACROSS, preferred_element_type=F32)
    ins, outs = ins.T, outs.T

    length_copy.wait()
    position = lax.broadcasted_iota(jnp.int32, (SEQ, ROUT), 0)
    kept = [jnp.where(position < lengths[s], outs[s * SEQ:(s + 1) * SEQ], 0.0) for s in range(NSEQ)]
    outs = jnp.concatenate(kept, axis=0).astype(BF)
    ins = jnp.concatenate([ins, ins], axis=1).astype(BF).astype(F32)
    own_slot = xlo * 8 + y * 2 + core
    for j in range(K // 128):
        a = lax.broadcasted_iota(jnp.int32, (ROUT, 128), 0)
        b = lax.broadcasted_iota(jnp.int32, (ROUT, 128), 1)
        pick = jnp.where(a == 2 * j + lax.div(b, RIN), 1.0, 0.0).astype(BF)
        wide = jnp.dot(outs, pick, preferred_element_type=F32)
        sums = jnp.sum((wide * ins).reshape(NP, 2 * SEQ, 128), axis=1)
        pg[own_slot, :, j * 128:(j + 1) * 128] = sums.astype(BF)

    p_copies = [go(pg.at[own_slot], p_send.at[j], p_recv.at[j], far(j)) for j in range(1, 8)]
    s_copies = [go(pg.at[own_slot], s_send.at[0], s_recv.at[0], sibling)]
    for j in range(1, 8):
        p_copies[j - 1].wait_recv()
        dy, dx = offset(j)
        slot = mod(xlo + dx, 2) * 8 + mod(y + 4 - dy, 4) * 2 + core
        s_copies.append(go(pg.at[slot], s_send.at[j], s_recv.at[j], sibling))
    own_f.wait()
    for copy in f_copies:
        copy.wait_recv()
    for copy in s_copies:
        copy.wait_recv()

    white = jnp.dot(pg[...].reshape(16 * NP, K), fcol[...].reshape(K, COLS), preferred_element_type=F32).astype(BF)
    qa[core, spot, member] = white[:HALF]
    qb[core, member, spot] = white[HALF:]

    a_far, b_near = [], []
    for j in range(1, 8):
        a_far.append(go(qa.at[core, spot, member], af_send.at[j], af_recv.at[j], far(j)))
        b_near.append(go(qb.at[core, member, spot], bn_send.at[j], bn_recv.at[j], near(j)))

    def ring(a, h):
        return mod(a + 4 - RING[h], 4)

    def a_batch(h):
        part = qa.at[core, spot, pl.ds(2 * ring(y, h), 2)]
        return [remote(part, an_send.at[h, j], an_recv.at[h, j], near(j)) for j in range(1, 8)]

    def b_batch(h):
        part = qb.at[core, member, pl.ds(2 * ring(z, h), 2)]
        return [remote(part, bf_send.at[h, j], bf_recv.at[h, j], far(j)) for j in range(1, 8)]

    def a_over(h):
        return remote(qa.at[core, :, pl.ds(2 * ring(y, h), 2)], ac_send.at[h], ac_recv.at[h], sibling)

    def b_over(h):
        return remote(qb.at[core, :, pl.ds(2 * ring(z, h), 2)], bc_send.at[h], bc_recv.at[h], sibling)

    a_batches, b_batches, overs = [], [], {}

    def send(h):
        for stage, batches, batch in ((a_far, a_batches, a_batch), (b_near, b_batches, b_batch)):
            for j in (2 * h, 2 * h + 1):
                if j:
                    stage[j - 1].wait_recv()
            batches.append(batch(h))
            for copy in batches[h]:
                copy.start()

    def hand(h):
        for name, batches, over in (("a", a_batches, a_over), ("b", b_batches, b_over)):
            for copy in batches[h]:
                copy.wait_recv()
            overs[name, h] = over(h)
            overs[name, h].start()

    def add(h):
        overs["a", h].wait_recv()
        at = ring(y, h)
        lhs = jnp.concatenate([qa[c, :, 2 * at + hi].reshape(8 * HALF, COLS) for hi in range(2) for c in range(2)], axis=1)
        cols = pl.ds(pl.multiple_of(at * 4 * COLS, 4 * COLS), 4 * COLS)
        for n in range(STORE // WIDE):
            some = slice(n * WIDE, (n + 1) * WIDE)
            part = lax.dot_general(lhs, store_v[some, cols], ACROSS, preferred_element_type=F32)
            if h == 0:
                total[:, some] = part
            elif h < 3:
                total[:, some] += part
            else:
                done[:, :, :, :, some] = (total[:, some] + part).astype(BF).reshape(4, 2, 4, SEQ, WIDE)

    send(0)
    send(1)
    hand(0)
    send(2)
    send(3)
    store_copy.wait()
    add(0)
    hand(1)
    add(1)
    hand(2)
    overs["b", 0].wait_recv()
    overs["b", 1].wait_recv()
    lhs = full_rows(qb, (ring(z, 0), ring(z, 1)))
    for n in range(STORE // WIDE):
        some = slice(n * WIDE, (n + 1) * WIDE)
        part = lax.dot_general(lhs, store_v[some, :], ACROSS, preferred_element_type=F32)
        early[:, :, :, some] = part.astype(BF).reshape(4, 4, SEQ, WIDE)
    hand(3)
    add(2)
    add(3)
    overs["b", 2].wait_recv()
    overs["b", 3].wait_recv()

    for copy in sends + [c for batch in a_batches + b_batches for c in batch] + list(overs.values()):
        copy.wait_send()


def full_rows(qb, ys):
    rows = [jnp.concatenate([qb[c, k, 2 * at + e] for k in range(8) for c in range(2)], axis=1) for at in ys for e in range(2)]
    return jnp.concatenate(rows, axis=0)


def score_kernel(qb, done, early, store, out, late, done_sem, early_sem, late_sem):
    z = lax.div(lax.axis_index("inner"), 4)
    zs = [mod(z + 4 - d, 4) for d in RING]
    copies = []
    for h in range(2):
        for hi in range(2):
            copies.append(pltpu.make_async_copy(early.at[2 * h + hi], out.at[:, 1, zs[h], hi], early_sem.at[h, hi]))
    for y in range(4):
        copies.append(pltpu.make_async_copy(done.at[:, :, y], out.at[y, 0], done_sem.at[y]))
    for copy in copies:
        copy.start()
    lhs = full_rows(qb, zs[2:])
    for n in range(STORE // WIDE):
        some = slice(n * WIDE, (n + 1) * WIDE)
        part = lax.dot_general(lhs, store[some, :], ACROSS, preferred_element_type=F32)
        late[:, :, :, some] = part.astype(BF).reshape(4, 4, SEQ, WIDE)
        for h in range(2):
            for hi in range(2):
                copy = pltpu.make_async_copy(late.at[2 * h + hi, :, :, some], out.at[:, 1, zs[2 + h], hi, :, some], late_sem.at[n, 2 * h + hi])
                copy.start()
                copies.append(copy)
    for copy in copies:
        copy.wait()


def shards(activations, out_grads, proj_in, proj_out, lengths, factor, store):
    dma = pltpu.SemaphoreType.DMA
    hbm = pl.BlockSpec(memory_space=pltpu.HBM)
    vmem = pl.BlockSpec(memory_space=pltpu.VMEM)
    parts = pl.pallas_call(
        gather_kernel,
        out_shape=[pltpu.VMEM((2, 8, 8, HALF, COLS), BF), pltpu.VMEM((4, 2, 4, SEQ, STORE), BF),
                   pltpu.VMEM((4, 4, SEQ, STORE), BF), pltpu.VMEM((STORE, K), BF)],
        in_specs=[hbm] * 7,
        out_specs=[vmem] * 4,
        scratch_shapes=[
            pltpu.VMEM((2, 8, 8, HALF, COLS), BF), pltpu.VMEM((8 * HALF, STORE), F32), pltpu.VMEM((2, 128, COLS), BF),
            pltpu.VMEM((TOK, D), BF), pltpu.VMEM((TOK, D), BF),
            pltpu.VMEM((RIN, D), BF), pltpu.VMEM((ROUT, D), BF),
            pltpu.VMEM((16, 128, COLS), BF), pltpu.VMEM((16, NP, K), BF), pltpu.SMEM((NSEQ,), jnp.int32),
            dma((NCHUNK, 4)), dma, dma, dma((2,)), dma, dma((16,)), dma((16,)),
        ] + [dma((8,))] * 8 + [dma((4, 8))] * 4 + [dma((4,))] * 4,
        compiler_params=pltpu.CompilerParams(collective_id=0, has_side_effects=True, vmem_limit_bytes=36 << 20),
        name="gather",
    )(*[pltpu.with_memory_space_constraint(v, pltpu.HBM)
        for v in (activations, out_grads, proj_in.T, proj_out.T, lengths, factor, store)])
    scores = pl.pallas_call(
        score_kernel,
        out_shape=jax.ShapeDtypeStruct((4, 2, 4, 2, SEQ, STORE), BF),
        in_specs=[vmem] * 4,
        out_specs=hbm,
        scratch_shapes=[pltpu.VMEM((4, 4, SEQ, STORE), BF), dma((4,)), dma((2, 2)), dma((STORE // WIDE, 4))],
        compiler_params=pltpu.CompilerParams(vmem_limit_bytes=24 << 20),
        name="score",
    )(*parts)
    return scores.reshape(16 * HALF, STORE)


def solution(mesh):
    in_specs = (
        P(("outer", "inner"), None),
        P(("outer", "inner"), None),
        P(),
        P(),
        P(("outer", "inner")),
        P("inner", None),
        P(("outer", "inner"), None),
    )
    out_specs = P(None, ("outer", "inner"))
    return jax.shard_map(shards, mesh=mesh, in_specs=in_specs, out_specs=out_specs, check_vma=False)
```

```python
import jax
import jax.numpy as jnp
from jax import lax
from jax.experimental import pallas as pl
from jax.experimental.pallas import tpu as pltpu
from jax.sharding import PartitionSpec as P

D = 8192
RIN = 64
ROUT = 32
K = 2048
SEQ = 16
TOK = 256
NSEQ = 16
NP = 8
COLS = 128
HALF = 64
CHUNK = 1024
NCHUNK = D // CHUNK
STORE = 3072
WIDE = 1024
BF = jnp.bfloat16
F32 = jnp.float32
MESH = pl.DeviceIdType.MESH
ACROSS = (((1,), (1,)), ((), ()))


def mod(a, b):
    return lax.rem(a, b)


RING = (0, 1, 3, 2)


def offset(j):
    return RING[j // 2], j % 2


def gather_kernel(act, grad, w_in, w_out, lengths_hbm, factor, store, qb, done, early, store_v,
                  qa, total, fown, act_v, grad_v, w_in_v, w_out_v, fcol, pg, lengths,
                  load_sem, store_sem, length_sem, stage_sem, own_f_sem, f_send, f_recv, p_send, p_recv, s_send, s_recv,
                  af_send, af_recv, bn_send, bn_recv, an_send, an_recv, bf_send, bf_recv,
                  ac_send, ac_recv, bc_send, bc_recv):
    outer = lax.axis_index("outer")
    inner = lax.axis_index("inner")
    core = mod(inner, 2)
    spot = lax.div(inner, 2)
    y, xlo = lax.div(outer, 2), mod(outer, 2)
    z, xhi = lax.div(spot, 2), mod(spot, 2)
    gx = mod(xlo + xhi, 2)
    sibling = (outer, spot * 2 + 1 - core)
    member = y * 2 + gx

    def near(j, flip=0):
        dz, dx = offset(j)
        hi = mod(xhi + dx, 2)
        return y * 2 + mod(gx + hi, 2), (mod(z + dz, 4) * 2 + hi) * 2 + mod(core + flip, 2)

    def far(j):
        dy, dx = offset(j)
        return mod(y + dy, 4) * 2 + mod(gx + dx + xhi, 2), inner

    length_copy = pltpu.make_async_copy(lengths_hbm, lengths, length_sem)
    length_copy.start()
    stages = []
    for n in range(2):
        cols = pl.ds(pl.multiple_of((member * 2 + n) * COLS, COLS), COLS)
        copy = pltpu.make_async_copy(factor.at[:, cols], fown.at[n], stage_sem.at[n])
        copy.start()
        stages.append(copy)
    loads = []
    for k in range(NCHUNK):
        cols = pl.ds(k * CHUNK, CHUNK)
        row = []
        for n, (src, dst) in enumerate(((w_in, w_in_v), (act, act_v), (w_out, w_out_v), (grad, grad_v))):
            copy = pltpu.make_async_copy(src.at[:, cols], dst.at[:, cols], load_sem.at[k, n])
            copy.start()
            row.append(copy)
        loads.append(row)

    barrier = pltpu.get_barrier_semaphore()
    peers = [near(j, flip) for j in range(8) for flip in range(2) if j + flip] + [far(j) for j in range(1, 8)]
    for peer in peers:
        pl.semaphore_signal(barrier, inc=1, device_id=peer, device_id_type=MESH)
    def remote(src, send, recv, target, dst=None):
        return pltpu.make_async_remote_copy(src_ref=src, dst_ref=src if dst is None else dst, send_sem=send, recv_sem=recv,
                                            device_id=target, device_id_type=MESH)

    sends = []

    def go(*args):
        copy = remote(*args)
        copy.start()
        sends.append(copy)
        return copy

    f_copies = []
    ins = jnp.zeros((RIN, TOK), F32)
    outs = jnp.zeros((ROUT, TOK), F32)
    for k in range(NCHUNK):
        cols = pl.ds(k * CHUNK, CHUNK)
        for copy in loads[k]:
            copy.wait()
        if k == 2:
            for copy in stages:
                copy.wait()
            pl.semaphore_wait(barrier, len(peers))
            for n in range(1, 16):
                to = near(n // 2, n % 2)
                f_copies.append(go(fown.at[mod(to[1], 2)], f_send.at[n], f_recv.at[n], to, fcol.at[inner]))
            own_f = pltpu.make_async_copy(fown.at[core], fcol.at[inner], own_f_sem)
            own_f.start()
        if k == NCHUNK - 1:
            store_copy = pltpu.make_async_copy(store, store_v, store_sem)
            store_copy.start()
        ins += lax.dot_general(w_in_v[:, cols], act_v[:, cols], ACROSS, preferred_element_type=F32)
        outs += lax.dot_general(w_out_v[:, cols], grad_v[:, cols], ACROSS, preferred_element_type=F32)
    ins, outs = ins.T, outs.T

    length_copy.wait()
    position = lax.broadcasted_iota(jnp.int32, (SEQ, ROUT), 0)
    kept = [jnp.where(position < lengths[s], outs[s * SEQ:(s + 1) * SEQ], 0.0) for s in range(NSEQ)]
    outs = jnp.concatenate(kept, axis=0).astype(BF)
    ins = jnp.concatenate([ins, ins], axis=1).astype(BF).astype(F32)
    own_slot = xlo * 8 + y * 2 + core
    for j in range(K // 128):
        a = lax.broadcasted_iota(jnp.int32, (ROUT, 128), 0)
        b = lax.broadcasted_iota(jnp.int32, (ROUT, 128), 1)
        pick = jnp.where(a == 2 * j + lax.div(b, RIN), 1.0, 0.0).astype(BF)
        wide = jnp.dot(outs, pick, preferred_element_type=F32)
        sums = jnp.sum((wide * ins).reshape(NP, 2 * SEQ, 128), axis=1)
        pg[own_slot, :, j * 128:(j + 1) * 128] = sums.astype(BF)

    p_copies = [go(pg.at[own_slot], p_send.at[j], p_recv.at[j], far(j)) for j in range(7, 0, -1)][::-1]
    s_copies = [go(pg.at[own_slot], s_send.at[0], s_recv.at[0], sibling)]
    for j in range(1, 8):
        p_copies[j - 1].wait_recv()
        dy, dx = offset(j)
        slot = mod(xlo + dx, 2) * 8 + mod(y + 4 - dy, 4) * 2 + core
        s_copies.append(go(pg.at[slot], s_send.at[j], s_recv.at[j], sibling))
    own_f.wait()
    for copy in f_copies:
        copy.wait_recv()
    for copy in s_copies:
        copy.wait_recv()

    white = jnp.dot(pg[...].reshape(16 * NP, K), fcol[...].reshape(K, COLS), preferred_element_type=F32).astype(BF)
    qa[core, spot, member] = white[:HALF]
    qb[core, member, spot] = white[HALF:]

    a_far, b_near = [], []
    for j in range(7, 0, -1):
        a_far.append(go(qa.at[core, spot, member], af_send.at[j], af_recv.at[j], far(j)))
        b_near.append(go(qb.at[core, member, spot], bn_send.at[j], bn_recv.at[j], near(j)))

    a_far.reverse()
    b_near.reverse()

    def ring(a, h):
        return mod(a + 4 - RING[h], 4)

    def a_batch(h):
        part = qa.at[core, spot, pl.ds(2 * ring(y, h), 2)]
        return [remote(part, an_send.at[h, j], an_recv.at[h, j], near(j)) for j in range(1, 8)]

    def b_batch(h):
        part = qb.at[core, member, pl.ds(2 * ring(z, h), 2)]
        return [remote(part, bf_send.at[h, j], bf_recv.at[h, j], far(j)) for j in range(1, 8)]

    def a_over(h):
        return remote(qa.at[core, :, pl.ds(2 * ring(y, h), 2)], ac_send.at[h], ac_recv.at[h], sibling)

    def b_over(h):
        return remote(qb.at[core, :, pl.ds(2 * ring(z, h), 2)], bc_send.at[h], bc_recv.at[h], sibling)

    a_batches, b_batches, overs = [], [], {}

    def send(h):
        for stage, batches, batch in ((a_far, a_batches, a_batch), (b_near, b_batches, b_batch)):
            for j in (2 * h, 2 * h + 1):
                if j:
                    stage[j - 1].wait_recv()
            batches.append(batch(h))
            for copy in batches[h]:
                copy.start()

    def hand(h):
        for name, batches, over in (("a", a_batches, a_over), ("b", b_batches, b_over)):
            for copy in batches[h]:
                copy.wait_recv()
            overs[name, h] = over(h)
            overs[name, h].start()

    def add(h):
        overs["a", h].wait_recv()
        at = ring(y, h)
        lhs = jnp.concatenate([qa[c, :, 2 * at + hi].reshape(8 * HALF, COLS) for hi in range(2) for c in range(2)], axis=1)
        cols = pl.ds(pl.multiple_of(at * 4 * COLS, 4 * COLS), 4 * COLS)
        for n in range(STORE // WIDE):
            some = slice(n * WIDE, (n + 1) * WIDE)
            part = lax.dot_general(lhs, store_v[some, cols], ACROSS, preferred_element_type=F32)
            if h == 0:
                total[:, some] = part
            elif h < 3:
                total[:, some] += part
            else:
                done[:, :, :, :, some] = (total[:, some] + part).astype(BF).reshape(4, 2, 4, SEQ, WIDE)

    send(0)
    send(1)
    hand(0)
    send(2)
    send(3)
    store_copy.wait()
    add(0)
    hand(1)
    add(1)
    hand(2)
    overs["b", 0].wait_recv()
    overs["b", 1].wait_recv()
    lhs = full_rows(qb, (ring(z, 0), ring(z, 1)))
    for n in range(STORE // WIDE):
        some = slice(n * WIDE, (n + 1) * WIDE)
        part = lax.dot_general(lhs, store_v[some, :], ACROSS, preferred_element_type=F32)
        early[:, :, :, some] = part.astype(BF).reshape(4, 4, SEQ, WIDE)
    hand(3)
    add(2)
    add(3)
    overs["b", 2].wait_recv()
    overs["b", 3].wait_recv()

    for copy in sends + [c for batch in a_batches + b_batches for c in batch] + list(overs.values()):
        copy.wait_send()


def full_rows(qb, ys):
    rows = [jnp.concatenate([qb[c, k, 2 * at + e] for k in range(8) for c in range(2)], axis=1) for at in ys for e in range(2)]
    return jnp.concatenate(rows, axis=0)


def score_kernel(qb, done, early, store, out, late, done_sem, early_sem, late_sem):
    z = lax.div(lax.axis_index("inner"), 4)
    zs = [mod(z + 4 - d, 4) for d in RING]
    copies = []
    for h in range(2):
        for hi in range(2):
            copies.append(pltpu.make_async_copy(early.at[2 * h + hi], out.at[:, 1, zs[h], hi], early_sem.at[h, hi]))
    for y in range(4):
        copies.append(pltpu.make_async_copy(done.at[:, :, y], out.at[y, 0], done_sem.at[y]))
    for copy in copies:
        copy.start()
    lhs = full_rows(qb, zs[2:])
    for n in range(STORE // WIDE):
        some = slice(n * WIDE, (n + 1) * WIDE)
        part = lax.dot_general(lhs, store[some, :], ACROSS, preferred_element_type=F32)
        late[:, :, :, some] = part.astype(BF).reshape(4, 4, SEQ, WIDE)
        for h in range(2):
            for hi in range(2):
                copy = pltpu.make_async_copy(late.at[2 * h + hi, :, :, some], out.at[:, 1, zs[2 + h], hi, :, some], late_sem.at[n, 2 * h + hi])
                copy.start()
                copies.append(copy)
    for copy in copies:
        copy.wait()


def shards(activations, out_grads, proj_in, proj_out, lengths, factor, store):
    dma = pltpu.SemaphoreType.DMA
    hbm = pl.BlockSpec(memory_space=pltpu.HBM)
    vmem = pl.BlockSpec(memory_space=pltpu.VMEM)
    parts = pl.pallas_call(
        gather_kernel,
        out_shape=[pltpu.VMEM((2, 8, 8, HALF, COLS), BF), pltpu.VMEM((4, 2, 4, SEQ, STORE), BF),
                   pltpu.VMEM((4, 4, SEQ, STORE), BF), pltpu.VMEM((STORE, K), BF)],
        in_specs=[hbm] * 7,
        out_specs=[vmem] * 4,
        scratch_shapes=[
            pltpu.VMEM((2, 8, 8, HALF, COLS), BF), pltpu.VMEM((8 * HALF, STORE), F32), pltpu.VMEM((2, 128, COLS), BF),
            pltpu.VMEM((TOK, D), BF), pltpu.VMEM((TOK, D), BF),
            pltpu.VMEM((RIN, D), BF), pltpu.VMEM((ROUT, D), BF),
            pltpu.VMEM((16, 128, COLS), BF), pltpu.VMEM((16, NP, K), BF), pltpu.SMEM((NSEQ,), jnp.int32),
            dma((NCHUNK, 4)), dma, dma, dma((2,)), dma, dma((16,)), dma((16,)),
        ] + [dma((8,))] * 8 + [dma((4, 8))] * 4 + [dma((4,))] * 4,
        compiler_params=pltpu.CompilerParams(collective_id=0, has_side_effects=True, vmem_limit_bytes=36 << 20),
        name="gather",
    )(*[pltpu.with_memory_space_constraint(v, pltpu.HBM)
        for v in (activations, out_grads, proj_in.T, proj_out.T, lengths, factor, store)])
    scores = pl.pallas_call(
        score_kernel,
        out_shape=jax.ShapeDtypeStruct((4, 2, 4, 2, SEQ, STORE), BF),
        in_specs=[vmem] * 4,
        out_specs=hbm,
        scratch_shapes=[pltpu.VMEM((4, 4, SEQ, STORE), BF), dma((4,)), dma((2, 2)), dma((STORE // WIDE, 4))],
        compiler_params=pltpu.CompilerParams(vmem_limit_bytes=24 << 20),
        name="score",
    )(*parts)
    return scores.reshape(16 * HALF, STORE)


def solution(mesh):
    in_specs = (
        P(("outer", "inner"), None),
        P(("outer", "inner"), None),
        P(),
        P(),
        P(("outer", "inner")),
        P("inner", None),
        P(("outer", "inner"), None),
    )
    out_specs = P(None, ("outer", "inner"))
    return jax.shard_map(shards, mesh=mesh, in_specs=in_specs, out_specs=out_specs, check_vma=False)
```
